256 devices in a mesh: fsdp: 32 (over y, z), dp: 8 (over x, core).
Axes of the slice: x: 4, y: 4, z: 8, core: 2. Of those that a mesh axis runs over, the one named last changes fastest.
Arguments:
- tokens: bfloat16 [103424, 768], P(('fsdp', 'dp')), may hold values from -6 to 6
- episodes: int32 [1024], P(('fsdp', 'dp')), may hold values from 0 to 3, as said below
- cotangent: bfloat16 [103424, 768], P(('fsdp', 'dp')), may hold values from -6 to 6
- inproj_master: float32 [768, 2304], P('fsdp'), may hold values from -0.21875 to 0.21875
- inproj_first: float32 [768, 2304], P('fsdp'), may hold values from -0.00390625 to 0.00390625
- inproj_second: float32 [768, 2304], P('fsdp'), may hold values from 1e-07 to 1e-06
- outproj_master: float32 [768, 768], P('fsdp'), may hold values from -2 to 2
- outproj_first: float32 [768, 768], P('fsdp'), may hold values from -0.00390625 to 0.00390625
- outproj_second: float32 [768, 768], P('fsdp'), may hold values from 1e-07 to 1e-06
- upproj_master: float32 [768, 3072], P('fsdp'), may hold values from -0.21875 to 0.21875
- upproj_first: float32 [768, 3072], P('fsdp'), may hold values from -0.00390625 to 0.00390625
- upproj_second: float32 [768, 3072], P('fsdp'), may hold values from 1e-07 to 1e-06
- downproj_master: float32 [3072, 768], P('fsdp'), may hold values from -0.109375 to 0.109375
- downproj_first: float32 [3072, 768], P('fsdp'), may hold values from -0.00390625 to 0.00390625
- downproj_second: float32 [3072, 768], P('fsdp'), may hold values from 1e-07 to 1e-06
- gains_master: float32 [2, 768], P(None, 'fsdp'), may hold values from 0.28 to 2.6
- gains_first: float32 [2, 768], P(None, 'fsdp'), may hold values from -0.00390625 to 0.00390625
- gains_second: float32 [2, 768], P(None, 'fsdp'), may hold values from 1e-07 to 1e-06
- biases_master: float32 [10, 768], P(None, 'fsdp'), may hold values from -0.875 to 0.875
- biases_first: float32 [10, 768], P(None, 'fsdp'), may hold values from -0.00390625 to 0.00390625
- biases_second: float32 [10, 768], P(None, 'fsdp'), may hold values from 1e-07 to 1e-06
Outputs:
- block_out: bfloat16 [103424, 768], P(('fsdp', 'dp'))
- input_grad: bfloat16 [103424, 768], P(('fsdp', 'dp'))
- grad_norm: float32 [], replicated
- inproj_grad: float32 [768, 2304], P('fsdp')
- inproj_weight: float32 [768, 2304], P('fsdp')
- inproj_mean: float32 [768, 2304], P('fsdp')
- inproj_square: float32 [768, 2304], P('fsdp')
- inproj_copy: bfloat16 [768, 2304], P('fsdp')
- outproj_grad: float32 [768, 768], P('fsdp')
- outproj_weight: float32 [768, 768], P('fsdp')
- outproj_mean: float32 [768, 768], P('fsdp')
- outproj_square: float32 [768, 768], P('fsdp')
- outproj_copy: bfloat16 [768, 768], P('fsdp')
- upproj_grad: float32 [768, 3072], P('fsdp')
- upproj_weight: float32 [768, 3072], P('fsdp')
- upproj_mean: float32 [768, 3072], P('fsdp')
- upproj_square: float32 [768, 3072], P('fsdp')
- upproj_copy: bfloat16 [768, 3072], P('fsdp')
- downproj_grad: float32 [3072, 768], P('fsdp')
- downproj_weight: float32 [3072, 768], P('fsdp')
- downproj_mean: float32 [3072, 768], P('fsdp')
- downproj_square: float32 [3072, 768], P('fsdp')
- downproj_copy: bfloat16 [3072, 768], P('fsdp')
- gains_grad: float32 [2, 768], P(None, 'fsdp')
- gains_step: float32 [2, 768], P(None, 'fsdp')
- gains_mean: float32 [2, 768], P(None, 'fsdp')
- gains_square: float32 [2, 768], P(None, 'fsdp')
- biases_grad: float32 [10, 768], P(None, 'fsdp')
- biases_weight: float32 [10, 768], P(None, 'fsdp')
- biases_mean: float32 [10, 768], P(None, 'fsdp')
- biases_square: float32 [10, 768], P(None, 'fsdp')
- biases_copy: bfloat16 [10, 768], P(None, 'fsdp')
- branch_bias_grad: float32 [768], P('fsdp')
The draws below stay inside these ranges and needn't reach their ends.
Inputs may be any that keep to these rules, and one draw needn't show every extreme that they name: Each aligned group of four views (views 4 i to 4 i + 3) is cut into episodes of consecutive views; every view holds the position in its group of its episode's first view, so the entry of a group's first view is 0, entries never fall within a group, and a view that starts an episode holds its own position. Some group is one episode of four views and some group is four episodes of one view.
All inputs are finite; a program needn't handle non-finite values.
Results may differ from the reference program's by a relative error of at most 0.035.
Values may be sent and summed in bfloat16 or wider, within the bound.
No kernel may reach another device: no remote copies, remote signals or barrier semaphores. Data moves between devices by JAX's collectives and lax.ppermute only.
A program may use at most 192 MiB of HBM per device.

```python
import math
import jax
import jax.numpy as jnp
import numpy as np
from jax import lax

D = 768
HEADS = 12
HEAD_DIM = 64
FF = 3072
PATCHES = 101
VIEWS = 1024
TOKENS = 103424


def draw_episodes(key, part):
    groups = VIEWS // 4
    layouts = jnp.asarray(np.array([[0, 1, 2, 3], [0, 1, 2, 2], [0, 1, 1, 3], [0, 0, 2, 3], [0, 0, 2, 2], [0, 1, 1, 1], [0, 0, 0, 3], [0, 0, 0, 0]], dtype=np.int32))
    bounds = jnp.asarray(np.array([1, 2, 3, 4, 6, 8, 10], dtype=np.int32))
    picked = jax.random.randint(key, (groups,), 0, 16)
    pattern = jnp.sum((picked[:, None] >= bounds[None, :]).astype(jnp.int32), axis=1)
    position = jnp.arange(groups)
    pattern = jnp.where(position == 0, 7, pattern)
    pattern = jnp.where(position == 1, 0, pattern)
    return layouts[pattern].reshape(VIEWS).astype(jnp.int32)


def draw_gains_master(key, part):
    where = jnp.arange(D, dtype=jnp.float32) / (D - 1)
    ramp = 0.5 + where
    rough = jax.random.uniform(key, (2, D), jnp.float32, 0.8, 1.2)
    return (ramp[None, :] * rough).astype(jnp.float32)


def levels(key, dims, shards, low, high):
    def one(dim, shards_of):
        draws = jax.random.uniform(jax.random.fold_in(jax.random.fold_in(key, 6), dim), (shards_of,), jnp.float32, low / len(shards), high / len(shards))
        return jnp.repeat(jnp.exp(draws), dims[dim] // shards_of).reshape((-1,) + (1,) * (len(dims) - dim - 1))

    level = one(*shards[0])
    for cut in shards[1:]:
        level = level * one(*cut)
    return level


def centred(own_key, shape, scale, most, cuts=(), kind=jnp.bfloat16):
    result = scale * jax.random.normal(own_key, shape, jnp.float32)
    if cuts:
        result = result * levels(own_key, shape, cuts, -0.22, 0.18)
    return jnp.clip(result, -most, most).astype(kind)


def setup_inputs(seed: int = 0) -> dict:
    key_list = jax.random.split(jax.random.key(seed), 22)
    return {
        "tokens": centred(key_list[0], (TOKENS, D), 1.0, 6.0, ((0, 256),)),
        "episodes": draw_episodes(jax.random.fold_in(key_list[21], 71), 0),
        "cotangent": centred(key_list[2], (TOKENS, D), 1.0, 6.0, ((0, 256),)),
        "inproj_master": centred(key_list[3], (D, 3 * D), D ** -0.5, 0.21875, ((0, 32),), jnp.float32),
        "inproj_first": centred(key_list[4], (D, 3 * D), 0.00075, 0.00390625, ((0, 32),), jnp.float32),
        "inproj_second": jnp.clip(jnp.exp(math.log(9.999999974752427e-07) - 2.3025851 * jax.random.uniform(key_list[5], (D, 3 * D), jnp.float32) ** levels(key_list[5], (D, 3 * D), ((0, 32),), -0.2, 0.2)), 1.0000000116860974e-07, 9.999999974752427e-07),
        "outproj_master": centred(key_list[6], (D, D), (D // 96) ** -0.5, 2.0, ((0, 32),), jnp.float32),
        "outproj_first": centred(key_list[7], (D, D), 0.00075, 0.00390625, ((0, 32),), jnp.float32),
        "outproj_second": jnp.clip(jnp.exp(math.log(9.999999974752427e-07) - 2.3025851 * jax.random.uniform(key_list[8], (D, D), jnp.float32) ** levels(key_list[8], (D, D), ((0, 32),), -0.2, 0.2)), 1.0000000116860974e-07, 9.999999974752427e-07),
        "upproj_master": centred(key_list[9], (D, FF), D ** -0.5, 0.21875, ((0, 32),), jnp.float32),
        "upproj_first": centred(key_list[10], (D, FF), 0.00075, 0.00390625, ((0, 32),), jnp.float32),
        "upproj_second": jnp.clip(jnp.exp(math.log(9.999999974752427e-07) - 2.3025851 * jax.random.uniform(key_list[11], (D, FF), jnp.float32) ** levels(key_list[11], (D, FF), ((0, 32),), -0.2, 0.2)), 1.0000000116860974e-07, 9.999999974752427e-07),
        "downproj_master": centred(key_list[12], (FF, D), FF ** -0.5, 0.109375, ((0, 32),), jnp.float32),
        "downproj_first": centred(key_list[13], (FF, D), 0.00075, 0.00390625, ((0, 32),), jnp.float32),
        "downproj_second": jnp.clip(jnp.exp(math.log(9.999999974752427e-07) - 2.3025851 * jax.random.uniform(key_list[14], (FF, D), jnp.float32) ** levels(key_list[14], (FF, D), ((0, 32),), -0.2, 0.2)), 1.0000000116860974e-07, 9.999999974752427e-07),
        "gains_master": draw_gains_master(jax.random.fold_in(key_list[21], 71), 0),
        "gains_first": centred(key_list[16], (2, D), 0.00075, 0.00390625, ((1, 32),), jnp.float32),
        "gains_second": jnp.clip(jnp.exp(math.log(9.999999974752427e-07) - 2.3025851 * jax.random.uniform(key_list[17], (2, D), jnp.float32) ** levels(key_list[17], (2, D), ((1, 32),), -0.2, 0.2)), 1.0000000116860974e-07, 9.999999974752427e-07),
        "biases_master": centred(key_list[18], (10, D), 0.15, 0.875, ((1, 32),), jnp.float32),
        "biases_first": centred(key_list[19], (10, D), 0.00075, 0.00390625, ((1, 32),), jnp.float32),
        "biases_second": jnp.clip(jnp.exp(math.log(9.999999974752427e-07) - 2.3025851 * jax.random.uniform(key_list[20], (10, D), jnp.float32) ** levels(key_list[20], (10, D), ((1, 32),), -0.2, 0.2)), 1.0000000116860974e-07, 9.999999974752427e-07),
    }


@jax.custom_vjp
def low(v):
    return lax.optimization_barrier(v.astype(jnp.bfloat16)).astype(jnp.float32)

@jax.custom_vjp
def low_back(v):
    return v

def low_keep(v):
    return (low(v), None)

def low_pass(kept, grad):
    return (grad,)

def back_keep(v):
    return (v, None)

def back_low(kept, grad):
    return (low(grad),)
low.defvjp(low_keep, low_pass)
low_back.defvjp(back_keep, back_low)
highest = lax.Precision.HIGHEST
norm_eps = 1e-06
neg_fill = -1e+30
clip_bound = 2.0
learn_rate = 0.07
decay_rate = 0.05
beta_first = 0.5
beta_second = 0.5
adam_eps = 1e-08
fix_first = 1.0 - beta_first ** 4
fix_second = 1.0 - beta_second ** 4

def matmul(left, right):
    return jnp.dot(left, right, precision=highest, preferred_element_type=jnp.float32)

def layer_norm(values, gain, shift):
    center = values - lax.optimization_barrier(jnp.mean(values, -1, keepdims=True))
    spread = lax.optimization_barrier(jnp.mean(center * center, -1, keepdims=True))
    return center * lax.rsqrt(spread + norm_eps) * gain + shift

def block_forward(rounded, block_rows, view_ids):
    in_weight, att_weight, up_weight, down_weight, gain_rows, bias_rows = rounded
    row_count = block_rows.shape[0]
    normed_one = low(layer_norm(block_rows, gain_rows[0], bias_rows[0]))
    qkv_bias = jnp.concatenate([bias_rows[2], jnp.zeros_like(bias_rows[2]), bias_rows[3]])
    qkv_rows = low(low_back(matmul(normed_one, in_weight) + qkv_bias))
    split_heads = qkv_rows.reshape(row_count, 3, HEADS, HEAD_DIM)
    query = split_heads[:, 0]
    keys = split_heads[:, 1]
    values = split_heads[:, 2]
    token_ids = jnp.repeat(view_ids, PATCHES)
    allowed = token_ids[:, None] == token_ids[None, :]
    scores = jnp.einsum('qhd,khd->hqk', query, keys, precision=highest) * HEAD_DIM ** (-0.5)
    scores = low_back(jnp.where(allowed[None], scores, neg_fill))
    row_max = lax.optimization_barrier(jnp.max(scores, -1, keepdims=True))
    exp_terms = jnp.exp(scores - row_max)
    prob_rows = low(exp_terms / lax.optimization_barrier(jnp.sum(exp_terms, -1, keepdims=True)))
    attended = jnp.einsum('hqk,khd->qhd', prob_rows, values, precision=highest).reshape(row_count, D)
    attended = low(low_back(attended))
    residual = block_rows + low_back(matmul(attended, att_weight) + bias_rows[4])
    normed_two = low(layer_norm(residual, gain_rows[1], bias_rows[1]))
    up_rows = low_back(matmul(normed_two, up_weight) + bias_rows[6:10].reshape(FF))
    hidden = low(jax.nn.gelu(up_rows, approximate=False))
    return residual + low_back(matmul(hidden, down_weight) + bias_rows[5])

def adam_step(master, first, second, grad, factor):
    clipped = grad * factor
    new_first = beta_first * first + (1.0 - beta_first) * clipped
    new_second = beta_second * second + (1.0 - beta_second) * clipped * clipped
    moved = new_first / fix_first / (jnp.sqrt(new_second / fix_second) + adam_eps)
    new_master = master - learn_rate * (moved + decay_rate * master)
    return (grad, new_master, new_first, new_second, new_master.astype(jnp.bfloat16))

def reference(tokens, episodes, cotangent, inproj_master, inproj_first, inproj_second, outproj_master, outproj_first, outproj_second, upproj_master, upproj_first, upproj_second, downproj_master, downproj_first, downproj_second, gains_master, gains_first, gains_second, biases_master, biases_first, biases_second):
    inputs = tokens.astype(jnp.float32)

    def forward(input_rows, in_w, att_w, up_w, down_w, gain_w, bias_w):
        rounded = (low(in_w), low(att_w), low(up_w), low(down_w), low(gain_w), low(bias_w))
        blocks = input_rows.reshape(-1, 4 * PATCHES, D)
        view_groups = episodes.reshape(-1, 4)
        step_fn = jax.checkpoint(lambda paired: block_forward(rounded, paired[0], paired[1]))
        return lax.map(step_fn, (blocks, view_groups)).reshape(-1, D)
    block_out, pullback = jax.vjp(forward, inputs, inproj_master, outproj_master, upproj_master, downproj_master, gains_master, biases_master)
    grads = pullback(cotangent.astype(jnp.float32))
    square_sum = sum((jnp.sum(grad_item * grad_item) for grad_item in grads[1:]))
    grad_norm = jnp.sqrt(square_sum)
    factor = jnp.minimum(1.0, clip_bound / grad_norm)
    upd_in = adam_step(inproj_master, inproj_first, inproj_second, grads[1], factor)
    upd_att = adam_step(outproj_master, outproj_first, outproj_second, grads[2], factor)
    upd_up = adam_step(upproj_master, upproj_first, upproj_second, grads[3], factor)
    upd_down = adam_step(downproj_master, downproj_first, downproj_second, grads[4], factor)
    upd_gain = adam_step(gains_master, gains_first, gains_second, grads[5], factor)
    upd_bias = adam_step(biases_master, biases_first, biases_second, grads[6], factor)
    gains_step = upd_gain[1] - gains_master
    return (block_out.astype(jnp.bfloat16), grads[0].astype(jnp.bfloat16), grad_norm, upd_in[0], upd_in[1], upd_in[2], upd_in[3], upd_in[4], upd_att[0], upd_att[1], upd_att[2], upd_att[3], upd_att[4], upd_up[0], upd_up[1], upd_up[2], upd_up[3], upd_up[4], upd_down[0], upd_down[1], upd_down[2], upd_down[3], upd_down[4], upd_gain[0], gains_step, upd_gain[2], upd_gain[3], upd_bias[0], upd_bias[1], upd_bias[2], upd_bias[3], upd_bias[4], grads[6][5])
```

```python
import functools

import jax
import jax.numpy as jnp
from jax import lax
from jax.experimental import pallas as pl
from jax.experimental.pallas import tpu as pltpu
from jax.sharding import Mesh
from jax.sharding import PartitionSpec as P

D = 768
HEADS = 12
FF = 3072
PATCHES = 101
ROWS = 4 * PATCHES
PAD = 416
SHARD = 24
DSHARD = 96
NY, NZ, NX, NC = 4, 8, 4, 2
AXES = ("y", "z", "x", "c")
SMALL = 128

norm_eps = 1e-06
neg_fill = -1e30
clip_bound = 2.0
learn_rate = 0.07
decay_rate = 0.05
beta_first = 0.5
beta_second = 0.5
adam_eps = 1e-08
fix_first = 1.0 - beta_first**4
fix_second = 1.0 - beta_second**4

f32 = jnp.float32
bf16 = jnp.bfloat16
VM = pl.BlockSpec(memory_space=pltpu.VMEM)
SM = pl.BlockSpec(memory_space=pltpu.SMEM)


def dot(a, b):
    return jnp.dot(a, b, preferred_element_type=f32)


def dot_t0(a, b):
    return lax.dot_general(a, b, (((0,), (0,)), ((), ())), preferred_element_type=f32)


def dot_t1(a, b):
    return lax.dot_general(a, b, (((1,), (1,)), ((), ())), preferred_element_type=f32)


def call(kernel, outs, ins, scratch=(), flops=0, smem=1):
    return pl.pallas_call(
        kernel,
        out_shape=[jax.ShapeDtypeStruct(s, d) for s, d in outs],
        in_specs=[SM] * smem + [VM] * (len(ins) - smem),
        out_specs=[VM] * len(outs),
        scratch_shapes=[pltpu.VMEM(s, d) for s, d in scratch],
        compiler_params=pltpu.CompilerParams(vmem_limit_bytes=56 * 1024 * 1024),
        cost_estimate=pl.CostEstimate(flops=flops, bytes_accessed=1 << 20, transcendentals=0),
    )(*ins)


def normed(v):
    center = v - jnp.mean(v, -1, keepdims=True)
    spread = jnp.mean(center * center, -1, keepdims=True)
    rstd = lax.rsqrt(spread + norm_eps)
    return center * rstd, rstd


def source_offset(core, k):
    other = (4, 7, 6, 5)[k]
    return k + core * (other - k)


def place_rows(pos, mine, other, dest):
    y, z, c = pos[0], pos[1], pos[3]
    for ky in range(NY):
        yb = lax.rem(y - ky + NY, NY)
        for refs, core in ((mine, c), (other, 1 - c)):
            for k in range(4):
                zb = lax.rem(z - source_offset(core, k) + NZ, NZ)
                start = pl.multiple_of((yb * NZ + zb) * SHARD, 8)
                dest[pl.ds(start, SHARD), :] = refs[ky][k].astype(f32)


def kernel_qkv(pos, ep, x_ref, m0, m1, m2, m3, o0, o1, o2, o3, w_ref, gb_ref, a1_ref, qkv_ref, att_ref, p_ref, wide, bias):
    place_rows(pos, (m0, m1, m2, m3), (o0, o1, o2, o3), wide)
    gb = wide[:, 3 * D :].T[:16]
    gb_ref[...] = gb

    def view_ids(dim):
        t = lax.broadcasted_iota(jnp.int32, (PAD, PAD), dim)
        ids = jnp.full((PAD, PAD), -1, jnp.int32)
        for v in (3, 2, 1, 0):
            ids = jnp.where(t < (v + 1) * PATCHES, ep[v], ids)
        return ids

    bias[...] = jnp.where(view_ids(0) == view_ids(1), 0.0, neg_fill).astype(f32)
    xhat, _ = normed(x_ref[...].astype(f32))
    a1 = (xhat * gb[0:1] + gb[2:3]).astype(bf16)
    a1_ref[...] = a1
    for part in range(3):
        shift = (gb[4:5], jnp.zeros((1, D), f32), gb[5:6])[part]
        for t in range(3):
            cols = pl.ds(part * D + t * 256, 256)
            w = wide[:, cols].astype(bf16)
            w_ref[:, cols] = w
            qkv_ref[:, cols] = (dot(a1_ref[...], w) + shift[:, t * 256 : (t + 1) * 256]).astype(bf16)

    low = lax.broadcasted_iota(jnp.int32, (PAD, 128), 1) < 64

    def pair(j, carry):
        lane = pl.multiple_of(j * 128, 128)
        q2 = qkv_ref[:, pl.ds(lane, 128)]
        k2 = qkv_ref[:, pl.ds(D + lane, 128)]
        v2 = qkv_ref[:, pl.ds(2 * D + lane, 128)]
        outs = []
        for h in range(2):
            keep = low if h == 0 else jnp.logical_not(low)
            qh = jnp.where(keep, q2.astype(f32) * 0.125, 0.0).astype(bf16)
            s = dot_t1(qh, k2) + bias[...]
            e = jnp.exp(s - jnp.max(s, -1, keepdims=True))
            p = (e * (1.0 / jnp.sum(e, -1, keepdims=True))).astype(bf16)
            p_ref[2 * j + h] = p
            outs.append(dot(p, v2))
        att_ref[:, pl.ds(lane, 128)] = jnp.where(low, outs[0], outs[1]).astype(bf16)
        return carry

    lax.fori_loop(0, HEADS // 2, pair, 0)


def kernel_up(
    pos, x_ref, gb_ref, att_ref, cot_ref, m0, m1, m2, m3, o0, o1, o2, o3, u0, u1, u2, u3, t0, t1, t2, t3,
    wo_ref, wu_ref, r1_ref, a2_ref, h_ref, g_ref, dm_ref, do_ref, wide,
):
    y, x, c = pos[0], pos[2], pos[3]
    place_rows(pos, (m0, m1, m2, m3), (o0, o1, o2, o3), wide)
    wo_ref[...] = wide[...].astype(bf16)
    for kx in range(NX):
        xb = lax.rem(x - kx + NX, NX)
        for refs, core in (((u0, u1, u2, u3), c), ((t0, t1, t2, t3), 1 - c)):
            start = pl.multiple_of((xb * 2 + core) * 384, 128)
            wu_ref[:, pl.ds(start, 384)] = refs[kx][...]
    gb = gb_ref[...]
    r1 = x_ref[...].astype(f32) + dot(att_ref[...], wo_ref[...]) + gb[6:7]
    r1_ref[...] = r1
    xhat, _ = normed(r1)
    a2_ref[...] = (xhat * gb[1:2] + gb[3:4]).astype(bf16)
    for t in range(12):
        cols = slice(t * 256, (t + 1) * 256)
        shift = gb_ref[8 + t // 3 : 9 + t // 3, (t % 3) * 256 : (t % 3 + 1) * 256]
        u = dot(a2_ref[...], wu_ref[:, cols]) + shift
        phi = 0.5 * (1.0 + lax.erf(u * 0.7071067811865476))
        h_ref[:, cols] = (u * phi).astype(bf16)
        g_ref[:, cols] = (phi + u * (jnp.exp(-0.5 * u * u) * 0.3989422804014327)).astype(bf16)

    def grad(j, carry):
        cols = pl.multiple_of(j * 384, 128)
        res = dot_t0(h_ref[:, pl.ds(cols, 384)], cot_ref[...]).astype(bf16)
        for s in range(4):
            yz = j * 4 + s
            at = lax.rem(yz, NZ) * NY + lax.rem(yz // NZ - y + NY, NY)
            lo = res[s * 96 : s * 96 + 48]
            hi = res[s * 96 + 48 : s * 96 + 96]

            @pl.when(c == 0)
            def _():
                dm_ref[at] = lo
                do_ref[at] = hi

            @pl.when(c == 1)
            def _():
                dm_ref[at] = hi
                do_ref[at] = lo

        return carry

    lax.fori_loop(0, 8, grad, 0)


def kernel_down_back(
    pos, gb_ref, cot_ref, g_ref, wm_ref, wot_ref, a2_ref, wu_ref, r1_ref,
    wd_ref, dr_ref, dz_ref, um_ref, uo_ref, sums_ref, du_ref, da_ref,
):
    x, c = pos[2], pos[3]
    for z in range(NZ):
        for yy in range(NY):
            base = (yy * NZ + z) * DSHARD
            wd_ref[pl.ds(pl.multiple_of(base + c * 48, 16), 48), :] = wm_ref[z, yy]
            wd_ref[pl.ds(pl.multiple_of(base + (1 - c) * 48, 16), 48), :] = wot_ref[z, yy]
    sums_ref[...] = jnp.zeros_like(sums_ref)
    for t in range(12):
        cols = slice(t * 256, (t + 1) * 256)
        dh = dot_t1(cot_ref[...], wd_ref[cols, :])
        du = (dh * g_ref[:, cols].astype(f32)).astype(bf16)
        du_ref[:, cols] = du
        sums_ref[8 + t // 3 : 9 + t // 3, (t % 3) * 256 : (t % 3 + 1) * 256] = jnp.sum(
            du.astype(f32), 0, keepdims=True
        )

    def grad(j, carry):
        res = dot_t0(a2_ref[...], du_ref[:, pl.ds(pl.multiple_of(j * 384, 128), 384)]).astype(bf16)
        at = lax.rem(j // 2 - x + NX, NX)

        @pl.when(lax.rem(j, 2) == c)
        def _():
            um_ref[at] = res

        @pl.when(lax.rem(j, 2) != c)
        def _():
            uo_ref[at] = res

        return carry

    lax.fori_loop(0, 8, grad, 0)
    for t in range(3):
        da_ref[:, t * 256 : (t + 1) * 256] = dot_t1(du_ref[...], wu_ref[t * 256 : (t + 1) * 256, :])
    gb = gb_ref[...]
    cot = cot_ref[...].astype(f32)
    xhat, rstd = normed(r1_ref[...])
    da = da_ref[...]
    e = da * gb[1:2]
    back = rstd * (e - jnp.mean(e, -1, keepdims=True) - xhat * jnp.mean(e * xhat, -1, keepdims=True))
    dr = cot + back
    dr_ref[...] = dr
    dz = dr.astype(bf16)
    dz_ref[...] = dz
    sums_ref[1:2, :] = jnp.sum(da * xhat, 0, keepdims=True)
    sums_ref[3:4, :] = jnp.sum(da, 0, keepdims=True)
    sums_ref[6:7, :] = jnp.sum(dz.astype(f32), 0, keepdims=True)
    sums_ref[7:8, :] = jnp.sum(cot, 0, keepdims=True)


def kernel_attention_back(
    pos, att_ref, dz_ref, wo_ref, qkv_ref, p_ref, a1_ref, wi_ref, x_ref, gb_ref, dr_ref, sums_ref,
    om_ref, oo_ref, im_ref, io_ref, ig_ref, datt_ref, dqkv_ref, da_ref, tall,
):
    y, c = pos[0], pos[3]

    def put(mine, other, res, half, cols):
        for yy in range(NY):
            at = lax.rem(yy - y + NY, NY)
            block = res[yy * 192 : (yy + 1) * 192]

            @pl.when(c == half)
            def _():
                mine[at, :, cols] = block

            @pl.when(c != half)
            def _():
                other[at, :, cols] = block

    for half in range(2):
        res = dot_t0(att_ref[...], dz_ref[:, half * 384 : (half + 1) * 384]).astype(bf16)
        put(om_ref, oo_ref, res, half, slice(0, 384))
    for t in range(3):
        cols = slice(t * 256, (t + 1) * 256)
        datt_ref[:, cols] = dot_t1(dz_ref[...], wo_ref[cols, :]).astype(bf16)

    low = lax.broadcasted_iota(jnp.int32, (PAD, 128), 1) < 64

    def pair(j, carry):
        lane = pl.multiple_of(j * 128, 128)
        q2 = qkv_ref[:, pl.ds(lane, 128)]
        k2 = qkv_ref[:, pl.ds(D + lane, 128)]
        v2 = qkv_ref[:, pl.ds(2 * D + lane, 128)]
        g2 = datt_ref[:, pl.ds(lane, 128)].astype(f32)
        o2 = att_ref[:, pl.ds(lane, 128)].astype(f32)
        parts = []
        for h in range(2):
            keep = low if h == 0 else jnp.logical_not(low)
            gh = jnp.where(keep, g2, 0.0)
            dot_rows = jnp.sum(gh * o2, -1, keepdims=True)
            gh = gh.astype(bf16)
            p = p_ref[2 * j + h]
            dp = dot_t1(gh, v2)
            ds = (p.astype(f32) * (dp - dot_rows)).astype(bf16)
            parts.append((dot(ds, k2), dot_t0(ds, q2), dot_t0(p, gh)))
        dq = jnp.where(low, parts[0][0], parts[1][0]) * 0.125
        dk = jnp.where(low, parts[0][1], parts[1][1]) * 0.125
        dv = parts[0][2] + parts[1][2]
        dqkv_ref[:, pl.ds(lane, 128)] = dq.astype(bf16)
        dqkv_ref[:, pl.ds(D + lane, 128)] = dk.astype(bf16)
        dqkv_ref[:, pl.ds(2 * D + lane, 128)] = dv.astype(bf16)
        return carry

    lax.fori_loop(0, HEADS // 2, pair, 0)

    for t in range(6):
        res = dot_t0(a1_ref[...], dqkv_ref[:, t * 384 : (t + 1) * 384]).astype(bf16)
        put(im_ref, io_ref, res, t // 3, slice((t % 3) * 384, (t % 3 + 1) * 384))
    for t in range(3):
        cols = slice(t * 256, (t + 1) * 256)
        da_ref[:, cols] = dot_t1(dqkv_ref[...], wi_ref[cols, :])
    gb = gb_ref[...]
    xhat, rstd = normed(x_ref[...].astype(f32))
    da = da_ref[...]
    e = da * gb[0:1]
    back = rstd * (e - jnp.mean(e, -1, keepdims=True) - xhat * jnp.mean(e * xhat, -1, keepdims=True))
    ig_ref[...] = (dr_ref[...] + back)[:ROWS].astype(bf16)
    tall[...] = jnp.zeros_like(tall)
    tall[0:16, :] = sums_ref[...]
    tall[0:1, :] = jnp.sum(da * xhat, 0, keepdims=True)
    tall[2:3, :] = jnp.sum(da, 0, keepdims=True)
    tall[4:5, :] = jnp.sum(dqkv_ref[:, :D].astype(f32), 0, keepdims=True)
    tall[5:6, :] = jnp.sum(dqkv_ref[:, 2 * D :].astype(f32), 0, keepdims=True)
    first = tall[...].T.astype(bf16)
    put(im_ref, io_ref, first, 0, slice(1152, 1280))
    tall[0:8, :] = tall[8:16, :]
    put(im_ref, io_ref, tall[...].T.astype(bf16), 1, slice(1152, 1280))


def kernel_block_out(r1_ref, h_ref, wd_ref, gb_ref, out_ref):
    out_ref[...] = (r1_ref[...] + dot(h_ref[...], wd_ref[...]) + gb_ref[7:8])[:ROWS].astype(bf16)


def shift(v, axis, k):
    n = dict(y=NY, z=NZ, x=NX)[axis]
    return lax.ppermute(v, axis, [(i, (i + k) % n) for i in range(n)])


def both_ways(v, axis, k):
    n = dict(y=NY, z=NZ, x=NX)[axis]
    pairs = []
    for i in range(n):
        pairs.append((2 * i, 2 * ((i + k) % n)))
        pairs.append((2 * i + 1, 2 * ((i - k) % n) + 1))
    return lax.ppermute(v, (axis, "c"), pairs)


def swap(v):
    return lax.ppermute(v, "c", [(0, 1), (1, 0)])


def gather4(v, axis):
    return [v] + [shift(v, axis, k) for k in (1, 2, 3)]


def scatter4(mine, other, axis):
    got = swap(other)
    held = [(mine[k].astype(f32) + got[k].astype(f32)) for k in range(4)]
    come = [shift(held[k].astype(bf16), axis, k) for k in (1, 2, 3)]
    return held[0] + come[0].astype(f32) + come[1].astype(f32) + come[2].astype(f32)


def square_total(grads):
    return sum((jnp.sum(grad_item * grad_item) for grad_item in grads))


def adam_step(master, first, second, grad, factor):
    clipped = grad * factor
    new_first = beta_first * first + (1.0 - beta_first) * clipped
    new_second = beta_second * second + (1.0 - beta_second) * clipped * clipped
    moved = new_first / fix_first / (jnp.sqrt(new_second / fix_second) + adam_eps)
    new_master = master - learn_rate * (moved + decay_rate * master)
    return (grad, new_master, new_first, new_second, new_master.astype(bf16))


def body(
    tokens, episodes, cotangent,
    inproj_master, inproj_first, inproj_second,
    outproj_master, outproj_first, outproj_second,
    upproj_master, upproj_first, upproj_second,
    downproj_master, downproj_first, downproj_second,
    gains_master, gains_first, gains_second,
    biases_master, biases_first, biases_second,
):
    y, z, x, c = (lax.axis_index(a) for a in AXES)
    pos = jnp.stack([y, z, x, c]).astype(jnp.int32)
    tok = jnp.pad(tokens, ((0, PAD - ROWS), (0, 0)))
    cot = jnp.pad(cotangent, ((0, PAD - ROWS), (0, 0)))

    small = jnp.concatenate([gains_master, biases_master], 0).T.astype(bf16)
    small = jnp.pad(small, ((0, 0), (0, SMALL - 12)))
    own = jnp.concatenate([inproj_master.astype(bf16), small, outproj_master.astype(bf16)], 1)
    far = lax.ppermute(own, ("z", "c"), [(2 * i + 1, 2 * ((i + 4) % NZ) + 1) for i in range(NZ)])
    near = [both_ways(own, "z", k) for k in (1, 2, 3)]
    stack = jnp.stack([jnp.where(c == 0, own, far)] + near)
    wide = 3 * D + SMALL
    wi_mine = gather4(stack[:, :, :wide], "y")
    wo_mine = gather4(stack[:, :, wide:], "y")
    wi_other = [swap(v) for v in wi_mine]
    wo_other = [swap(v) for v in wo_mine]

    piece = lax.dynamic_slice(upproj_master, (0, (x * 2 + c) * 384), (SHARD, 384)).astype(bf16)
    piece = jnp.broadcast_to(piece[None], (NY * NZ, SHARD, 384))
    piece = lax.all_to_all(piece, ("y", "z"), split_axis=0, concat_axis=0, tiled=True)
    wu_mine = gather4(piece.reshape(D, 384), "x")
    wu_other = [swap(v) for v in wu_mine]

    part = lax.dynamic_slice(downproj_master, (c * 48, 0), (48, D)).astype(bf16)
    wd_mine = lax.all_gather(part, "y", axis=0)
    wd_mine = lax.all_gather(wd_mine, "z", axis=0)
    wd_other = swap(wd_mine)

    wi, gb, a1, qkv, att, probs = call(
        kernel_qkv,
        [((D, 3 * D), bf16), ((16, D), f32), ((PAD, D), bf16), ((PAD, 3 * D), bf16), ((PAD, D), bf16),
         ((HEADS, PAD, PAD), bf16)],
        [pos, episodes, tok, *wi_mine, *wi_other],
        [((D, wide), f32), ((PAD, PAD), f32)],
        flops=8 * 10**9, smem=2,
    )
    wo, wu, r1, a2, h, g, dm, do = call(
        kernel_up,
        [((D, D), bf16), ((D, FF), bf16), ((PAD, D), f32), ((PAD, D), bf16), ((PAD, FF), bf16), ((PAD, FF), bf16),
         ((NY * NZ, 48, D), bf16), ((NY * NZ, 48, D), bf16)],
        [pos, tok, gb, att, cot, *wo_mine, *wo_other, *wu_mine, *wu_other],
        [((D, D), f32)],
        flops=10 * 10**9,
    )
    wd, dr, dz, um, uo, sums = call(
        kernel_down_back,
        [((FF, D), bf16), ((PAD, D), f32), ((PAD, D), bf16), ((NX, D, 384), bf16), ((NX, D, 384), bf16), ((16, D), f32)],
        [pos, gb, cot, g, wd_mine, wd_other, a2, wu, r1],
        [((PAD, FF), bf16), ((PAD, D), f32)],
        flops=8 * 10**9,
    )
    om, oo, im, io, input_grad = call(
        kernel_attention_back,
        [((NY, 192, 384), bf16), ((NY, 192, 384), bf16), ((NY, 192, 1280), bf16), ((NY, 192, 1280), bf16),
         ((ROWS, D), bf16)],
        [pos, att, dz, wo, qkv, probs, a1, wi, tok, gb, dr, sums],
        [((PAD, D), bf16), ((PAD, 3 * D), bf16), ((PAD, D), f32), ((SMALL, D), f32)],
        flops=16 * 10**9,
    )
    (block_out,) = call(
        kernel_block_out, [((ROWS, D), bf16)], [r1, h, wd, gb], flops=2 * 10**9, smem=0
    )

    down = (dm.astype(f32) + swap(do).astype(f32)).astype(bf16)
    down = lax.psum_scatter(down, "z", scatter_dimension=0, tiled=True)
    come = [shift(down[k], "y", k) for k in (1, 2, 3)]
    down = (down[0].astype(f32) + come[0].astype(f32) + come[1].astype(f32) + come[2].astype(f32)).astype(bf16)

    up = scatter4(um, uo, "x").astype(bf16).reshape(NY * NZ, SHARD, 384)
    up = lax.all_to_all(up, ("y", "z"), split_axis=0, concat_axis=0, tiled=True)
    up = jnp.sum(up.astype(f32), 0).astype(bf16)

    out = scatter4(om, oo, "y").astype(bf16)
    inn = scatter4(im, io, "y").astype(bf16)
    both = jnp.concatenate([inn, out], 1).reshape(NZ, SHARD, 1280 + 384)
    both = lax.all_to_all(both, "z", split_axis=0, concat_axis=0, tiled=True)
    both = jnp.sum(both.astype(f32), 0).astype(bf16)
    pack = jnp.concatenate([both, up, down.reshape(SHARD, 2 * D)], 1)
    packs = gather4(pack, "x")
    total = sum(v.astype(f32) for v in packs)
    mine = jnp.concatenate([total[:, :1664], total[:, 2048:]], 1).astype(bf16)
    ups = jnp.stack([v[:, 1664:2048] for v in packs])
    ups = jnp.take(ups, jnp.mod(x - jnp.arange(NX), NX), axis=0)
    send = jnp.concatenate([mine] + [ups[k] for k in range(NX)], 1)
    recv = swap(send)
    lo = jnp.where(c == 0, send, recv).astype(f32)
    hi = jnp.where(c == 0, recv, send).astype(f32)
    in_grad = jnp.concatenate([lo[:, :1152], hi[:, :1152]], 1)
    out_grad = jnp.concatenate([lo[:, 1280:1664], hi[:, 1280:1664]], 1)
    at = 1664 + 2 * D
    up_grad = jnp.concatenate(
        [v[:, at + 384 * k : at + 384 * (k + 1)] for k in range(NX) for v in (lo, hi)], 1
    )
    down_grad = jnp.concatenate([v[:, 1664:at].reshape(48, D) for v in (lo, hi)], 0)
    tiny = jnp.concatenate([lo[:, 1152:1160], hi[:, 1152:1156]], 1).T
    gain_grad = tiny[:2]
    bias_grad = tiny[2:12]
    summed = (in_grad, out_grad, up_grad, down_grad, gain_grad, bias_grad)

    local = jnp.full((NY * NZ, 8, 128), square_total(summed), f32)
    local = lax.all_to_all(local, ("y", "z"), split_axis=0, concat_axis=0, tiled=True)
    square_sum = jnp.sum(local[:, 0, 0])
    grad_norm = jnp.sqrt(square_sum)
    factor = jnp.minimum(1.0, clip_bound / grad_norm)
    upd_in = adam_step(inproj_master, inproj_first, inproj_second, summed[0], factor)
    upd_att = adam_step(outproj_master, outproj_first, outproj_second, summed[1], factor)
    upd_up = adam_step(upproj_master, upproj_first, upproj_second, summed[2], factor)
    upd_down = adam_step(downproj_master, downproj_first, downproj_second, summed[3], factor)
    upd_gain = adam_step(gains_master, gains_first, gains_second, summed[4], factor)
    upd_bias = adam_step(biases_master, biases_first, biases_second, summed[5], factor)
    return (
        block_out, input_grad, grad_norm,
        *upd_in, *upd_att, *upd_up, *upd_down,
        upd_gain[0], upd_gain[1] - gains_master, upd_gain[2], upd_gain[3],
        *upd_bias,
        bias_grad[5],
    )


def solution(mesh):
    fine = Mesh(mesh.devices.reshape(NY, NZ, NX, NC), AXES)
    rows, own, own_cols = P(AXES, None), P(("y", "z"), None), P(None, ("y", "z"))
    in_specs = (rows, P(AXES), rows) + (own,) * 12 + (own_cols,) * 6
    out_specs = (rows, rows, P()) + (own,) * 20 + (own_cols,) * 9 + (P(("y", "z")),)
    return jax.shard_map(body, mesh=fine, in_specs=in_specs, out_specs=out_specs, check_vma=False)
```

```python
import functools

import jax
import jax.numpy as jnp
from jax import lax
from jax.experimental import pallas as pl
from jax.experimental.pallas import tpu as pltpu
from jax.sharding import Mesh
from jax.sharding import PartitionSpec as P

D = 768
HEADS = 12
FF = 3072
PATCHES = 101
ROWS = 4 * PATCHES
PAD = 416
SHARD = 24
DSHARD = 96
NY, NZ, NX, NC = 4, 8, 4, 2
AXES = ("y", "z", "x", "c")
SMALL = 128

norm_eps = 1e-06
neg_fill = -1e30
clip_bound = 2.0
learn_rate = 0.07
decay_rate = 0.05
beta_first = 0.5
beta_second = 0.5
adam_eps = 1e-08
fix_first = 1.0 - beta_first**4
fix_second = 1.0 - beta_second**4

f32 = jnp.float32
bf16 = jnp.bfloat16
VM = pl.BlockSpec(memory_space=pltpu.VMEM)
SM = pl.BlockSpec(memory_space=pltpu.SMEM)


def dot(a, b):
    return jnp.dot(a, b, preferred_element_type=f32)


def dot_t0(a, b):
    return lax.dot_general(a, b, (((0,), (0,)), ((), ())), preferred_element_type=f32)


def dot_t1(a, b):
    return lax.dot_general(a, b, (((1,), (1,)), ((), ())), preferred_element_type=f32)


def added(*parts):
    return sum(p.astype(f32) for p in parts).astype(bf16)


def call(kernel, outs, ins, scratch=(), smem=1, flops=1000, late=(), early=(), extra=0, kept=(), held=()):
    streamed = len(late) + len(early)
    n_in, n_out = len(ins), len(outs)

    def wrapped(*refs):
        ins_r, outs_r = list(refs[:n_in]), list(refs[n_in : n_in + n_out])
        rest = list(refs[n_in + n_out :])
        sems = rest.pop()
        own = rest.pop() if extra else None
        bufs = rest[len(scratch) :]
        arriving, leaving = {}, {}
        for k, i in enumerate(late):
            copy = pltpu.make_async_copy(ins_r[i], bufs[k], sems.at[k])
            copy.start()
            ins_r[i] = bufs[k]
            arriving[id(bufs[k])] = copy
        for k, i in enumerate(early):
            buf = bufs[len(late) + k]
            leaving[id(buf)] = [pltpu.make_async_copy(buf, outs_r[i], sems.at[len(late) + k]), False]
            outs_r[i] = buf

        def need(ref):
            arriving.pop(id(ref)).wait()

        def flush(ref):
            leaving[id(ref)][0].start()
            leaving[id(ref)][1] = True

        kernel(*ins_r, *outs_r, *rest[: len(scratch)], *([own] if extra else []), need, flush)
        for copy, started in leaving.values():
            if not started:
                copy.start()
        for copy, _ in leaving.values():
            copy.wait()

    any_place = pl.BlockSpec(memory_space=pl.ANY)
    return pl.pallas_call(
        wrapped if streamed else kernel,
        out_shape=[jax.ShapeDtypeStruct(s, d) for s, d in outs],
        in_specs=[SM if i < smem else any_place if i in late + kept else VM for i in range(n_in)],
        out_specs=[any_place if i in early + held else VM for i in range(n_out)],
        scratch_shapes=[pltpu.VMEM(s, d) for s, d in scratch]
        + [pltpu.VMEM(ins[i].shape, ins[i].dtype) for i in late]
        + [pltpu.VMEM(*outs[i]) for i in early]
        + ([pltpu.SemaphoreType.DMA((extra,))] if extra else [])
        + ([pltpu.SemaphoreType.DMA((streamed,))] if streamed else []),
        compiler_params=pltpu.CompilerParams(vmem_limit_bytes=56 * 1024 * 1024),
        cost_estimate=pl.CostEstimate(flops=flops, bytes_accessed=1000, transcendentals=0),
    )(*ins)


def normed(v):
    center = v - jnp.mean(v, -1, keepdims=True)
    spread = jnp.mean(center * center, -1, keepdims=True)
    rstd = lax.rsqrt(spread + norm_eps)
    return center * rstd, rstd


def source_offset(core, k):
    other = (4, 7, 6, 5)[k]
    return k + core * (other - k)


def row_bias(gb, row, t):
    return gb[row : row + 1, t * 256 : (t + 1) * 256]


def kernel_attention(
    pos, ep, x_ref, m0, m1, m2, m3, o0, o1, o2, o3,
    w_ref, wo_ref, gb_ref, a1_ref, qkv_ref, att_ref, p_out, r1_ref, a2_ref, wide, bias, p_ref, p_sems, need, flush,
):
    y, z, c = pos[0], pos[1], pos[3]
    for refs, core in (((m0, m1, m2, m3), c), ((o0, o1, o2, o3), 1 - c)):
        for k in range(4):
            zb = lax.rem(z - source_offset(core, k) + NZ, NZ)
            for ky in range(NY):
                yb = lax.rem(y - ky + NY, NY)
                start = pl.multiple_of((yb * NZ + zb) * SHARD, 8)
                wide[pl.ds(start, SHARD), :] = refs[ky][k].astype(f32)
    gb = wide[:, 3 * D : 3 * D + SMALL].T[:16]
    gb_ref[...] = gb

    def view_ids(dim):
        t = lax.broadcasted_iota(jnp.int32, (PAD, PAD), dim)
        ids = jnp.full((PAD, PAD), -1, jnp.int32)
        for v in (3, 2, 1, 0):
            ids = jnp.where(t < (v + 1) * PATCHES, ep[v], ids)
        return ids

    bias[...] = jnp.where(view_ids(0) == view_ids(1), 0.0, neg_fill).astype(f32)
    x = x_ref[...].astype(f32)
    xhat, _ = normed(x)
    a1_ref[...] = (xhat * gb[0:1] + gb[2:3]).astype(bf16)
    for part in range(3):
        for t in range(3):
            cols = pl.ds(part * D + t * 256, 256)
            w = wide[:, cols].astype(bf16)
            w_ref[:, cols] = w
            res = dot(a1_ref[...], w)
            if part != 1:
                res = res + row_bias(gb, 4 if part == 0 else 5, t)
            qkv_ref[:, cols] = res.astype(bf16)
    for ref in (w_ref, a1_ref, qkv_ref):
        flush(ref)
    wo_ref[...] = wide[:, 3 * D + SMALL :].astype(bf16)
    flush(wo_ref)

    def p_copy(j):
        two = pl.ds(2 * j, 2)
        return pltpu.make_async_copy(p_ref.at[two], p_out.at[two], p_sems.at[j])

    low = lax.broadcasted_iota(jnp.int32, (PAD, 128), 1) < 64

    def pair(j, carry):
        lane = pl.multiple_of(j * 128, 128)
        q2 = qkv_ref[:, pl.ds(lane, 128)]
        k2 = qkv_ref[:, pl.ds(D + lane, 128)]
        v2 = qkv_ref[:, pl.ds(2 * D + lane, 128)]
        outs = []
        for h in range(2):
            keep = low if h == 0 else jnp.logical_not(low)
            qh = jnp.where(keep, q2.astype(f32) * 0.125, 0.0).astype(bf16)
            s = dot_t1(qh, k2) + bias[...]
            e = jnp.exp(s - jnp.max(s, -1, keepdims=True))
            p = (e * (1.0 / jnp.sum(e, -1, keepdims=True))).astype(bf16)
            p_ref[2 * j + h] = p
            outs.append(dot(p, v2))
        att_ref[:, pl.ds(lane, 128)] = jnp.where(low, outs[0], outs[1]).astype(bf16)
        p_copy(j).start()
        return carry

    lax.fori_loop(0, HEADS // 2, pair, 0)
    flush(att_ref)
    r1 = x + dot(att_ref[...], wo_ref[...]) + gb[6:7]
    r1_ref[...] = r1
    xhat, _ = normed(r1)
    a2_ref[...] = (xhat * gb[1:2] + gb[3:4]).astype(bf16)
    for j in range(HEADS // 2):
        p_copy(j).wait()


def kernel_up(
    pos, gb_ref, cot_ref, a2_ref, own, near, near_o, far, far_o, wu_ref, h_ref, g_ref, dm_ref, do_ref, need, flush
):
    x, c = pos[2], pos[3]
    prev, succ = lax.rem(x + 3 + 2 * c, NX), lax.rem(x + 5 - 2 * c, NX)
    for ref, blocks in (
        (own, ((x, c), (x, 1 - c))),
        (near, ((prev, c), (prev, 1 - c))),
        (near_o, ((succ, 1 - c), (succ, c))),
        (far, ((lax.rem(x + 2, NX), c),)),
        (far_o, ((lax.rem(x + 2, NX), 1 - c),)),
    ):
        need(ref)
        for i, (xb, core) in enumerate(blocks):
            cols = pl.ds(pl.multiple_of((xb * 2 + core) * 384, 128), 384)
            wu_ref[:, cols] = ref[i] if len(blocks) == 2 else ref[...]
    flush(wu_ref)
    for t in range(12):
        cols = slice(t * 256, (t + 1) * 256)
        u = dot(a2_ref[...], wu_ref[:, cols]) + row_bias(gb_ref, 8 + t // 3, t % 3)
        phi = 0.5 * (1.0 + lax.erf(u * 0.7071067811865476))
        h_ref[:, cols] = (u * phi).astype(bf16)
        g_ref[:, cols] = (phi + u * (jnp.exp(-0.5 * u * u) * 0.3989422804014327)).astype(bf16)

    flush(h_ref)
    flush(g_ref)
    need(cot_ref)

    def grad(j, carry):
        res = dot_t0(h_ref[:, pl.ds(pl.multiple_of(j * 384, 128), 384)], cot_ref[...])
        for s in range(4):
            for xx in range(NX):
                block = res[s * 96 + xx * 24 : s * 96 + xx * 24 + 24].astype(bf16)

                @pl.when(c == 0)
                def _():
                    dm_ref[xx, j * 4 + s] = block[:, :384]
                    do_ref[xx, j * 4 + s] = block[:, 384:]

                @pl.when(c == 1)
                def _():
                    dm_ref[xx, j * 4 + s] = block[:, 384:]
                    do_ref[xx, j * 4 + s] = block[:, :384]

        return carry

    lax.fori_loop(0, 8, grad, 0)


def kernel_down_back(
    pos, cot_ref, g_ref, wm_ref, wt_ref, a2_ref, wd_ref, um_ref, uo_ref, du_ref, sums_ref, need, flush,
):
    y, c = pos[0], pos[3]

    def rows(yz, carry):
        for ref, core in ((wm_ref, c), (wt_ref, 1 - c)):
            cols = pl.ds(pl.multiple_of(core * 384, 128), 384)
            for p in range(2):
                block = jnp.concatenate([ref[2 * p, yz].astype(f32), ref[2 * p + 1, yz].astype(f32)], 0)
                wd_ref[pl.ds(pl.multiple_of(yz * DSHARD + p * 48, 16), 48), cols] = block.astype(bf16)
        return carry

    lax.fori_loop(0, NY * NZ, rows, 0)
    flush(wd_ref)
    sums_ref[...] = jnp.zeros_like(sums_ref)
    need(cot_ref)
    need(g_ref)
    for t in range(12):
        cols = slice(t * 256, (t + 1) * 256)
        dh = dot_t1(cot_ref[...], wd_ref[cols, :])
        du = (dh * g_ref[:, cols].astype(f32)).astype(bf16)
        du_ref[:, cols] = du
        sums_ref[8 + t // 3 : 9 + t // 3, (t % 3) * 256 : (t % 3 + 1) * 256] = jnp.sum(
            du.astype(f32), 0, keepdims=True
        )

    flush(du_ref)
    need(a2_ref)

    def grad(j, carry):
        res = dot_t0(a2_ref[...], du_ref[:, pl.ds(pl.multiple_of(j * 384, 128), 384)]).astype(bf16)
        put_rows(y, c, um_ref, uo_ref, res, lax.rem(j, 2), pl.ds(pl.multiple_of((j // 2) * 384, 128), 384))
        return carry

    lax.fori_loop(0, 8, grad, 0)


def put_rows(y, c, mine, other, res, half, cols):
    for yy in range(NY):
        block = res[yy * 192 : (yy + 1) * 192]
        at = lax.rem(yy - y + NY, NY)

        @pl.when(c == half)
        def _():
            mine[at, :, cols] = block

        @pl.when(c != half)
        def _():
            other[at, :, cols] = block


def kernel_mid_back(
    pos, gb_ref, cot_ref, du_ref, wu_ref, r1_ref, sums_in, att_ref, wo_ref, qkv_ref, p_in,
    dr_ref, om_ref, oo_ref, dqkv_ref, sums_ref, da_ref, dz_ref, datt_ref, p_ref, p_sems, need, flush,
):
    y, c = pos[0], pos[3]

    def p_copy(j):
        two = pl.ds(2 * j, 2)
        return pltpu.make_async_copy(p_in.at[two], p_ref.at[two], p_sems.at[j])

    for j in range(HEADS // 2):
        p_copy(j).start()
    need(du_ref)
    need(wu_ref)
    for t in range(3):
        da_ref[:, t * 256 : (t + 1) * 256] = dot_t1(du_ref[...], wu_ref[t * 256 : (t + 1) * 256, :])
    gb = gb_ref[...]
    need(cot_ref)
    need(r1_ref)
    cot = cot_ref[...].astype(f32)
    xhat, rstd = normed(r1_ref[...])
    da = da_ref[...]
    e = da * gb[1:2]
    back = rstd * (e - jnp.mean(e, -1, keepdims=True) - xhat * jnp.mean(e * xhat, -1, keepdims=True))
    dr = cot + back
    dr_ref[...] = dr
    flush(dr_ref)
    dz = dr.astype(bf16)
    dz_ref[...] = dz
    sums_ref[...] = sums_in[...]
    sums_ref[1:2, :] = jnp.sum(da * xhat, 0, keepdims=True)
    sums_ref[3:4, :] = jnp.sum(da, 0, keepdims=True)
    sums_ref[6:7, :] = jnp.sum(dz.astype(f32), 0, keepdims=True)
    sums_ref[7:8, :] = jnp.sum(cot, 0, keepdims=True)
    need(att_ref)
    for half in range(2):
        res = dot_t0(att_ref[...], dz_ref[:, half * 384 : (half + 1) * 384]).astype(bf16)
        put_rows(y, c, om_ref, oo_ref, res, half, slice(0, 384))
    flush(om_ref)
    flush(oo_ref)
    need(wo_ref)
    for t in range(3):
        cols = slice(t * 256, (t + 1) * 256)
        datt_ref[:, cols] = dot_t1(dz_ref[...], wo_ref[cols, :]).astype(bf16)
    need(qkv_ref)
    low = lax.broadcasted_iota(jnp.int32, (PAD, 128), 1) < 64

    def pair(j, carry):
        lane = pl.multiple_of(j * 128, 128)
        p_copy(j).wait()
        q2 = qkv_ref[:, pl.ds(lane, 128)]
        k2 = qkv_ref[:, pl.ds(D + lane, 128)]
        v2 = qkv_ref[:, pl.ds(2 * D + lane, 128)]
        g2 = datt_ref[:, pl.ds(lane, 128)].astype(f32)
        o2 = att_ref[:, pl.ds(lane, 128)].astype(f32)
        parts = []
        for h in range(2):
            keep = low if h == 0 else jnp.logical_not(low)
            gh = jnp.where(keep, g2, 0.0)
            dot_rows = jnp.sum(gh * o2, -1, keepdims=True)
            gh = gh.astype(bf16)
            p = p_ref[2 * j + h]
            ds = (p.astype(f32) * (dot_t1(gh, v2) - dot_rows)).astype(bf16)
            parts.append((dot(ds, k2), dot_t0(ds, q2), dot_t0(p, gh)))
        dq = jnp.where(low, parts[0][0], parts[1][0]) * 0.125
        dk = jnp.where(low, parts[0][1], parts[1][1]) * 0.125
        dv = parts[0][2] + parts[1][2]
        dqkv_ref[:, pl.ds(lane, 128)] = dq.astype(bf16)
        dqkv_ref[:, pl.ds(D + lane, 128)] = dk.astype(bf16)
        dqkv_ref[:, pl.ds(2 * D + lane, 128)] = dv.astype(bf16)
        return carry

    lax.fori_loop(0, HEADS // 2, pair, 0)


def kernel_in_grad(
    pos, dqkv_ref, a1_ref, blocks, u0, u1, u2, u3, im_ref, io_ref, down_ref, up_ref, need, flush
):
    y, c = pos[0], pos[3]
    for t in range(6):
        res = dot_t0(a1_ref[...], dqkv_ref[:, t * 384 : (t + 1) * 384]).astype(bf16)
        put_rows(y, c, im_ref, io_ref, res, t // 3, slice((t % 3) * 384, (t % 3 + 1) * 384))
    flush(im_ref)
    flush(io_ref)
    need(blocks)
    for t in range(8):
        rows = slice(t * 96, (t + 1) * 96)
        down_ref[rows, :] = added(*(blocks[k, rows, :] for k in range(NX)))
    flush(down_ref)
    for u in (u0, u1, u2, u3):
        need(u)
    for k in range(NX):
        cols = slice(k * 384, (k + 1) * 384)
        total = sum(u[:, cols].astype(f32) for u in (u0, u1, u2, u3))
        for zz in range(NZ):
            up_ref[zz * NX + k] = total[zz * SHARD : (zz + 1) * SHARD].astype(bf16)


def kernel_input_grad(
    pos, dqkv_ref, wi_ref, x_ref, gb_ref, dr_ref, sums_ref, sm_ref, so_ref, ig_ref, da_ref, tall, need, flush,
):
    y, c = pos[0], pos[3]
    for t in range(3):
        cols = slice(t * 256, (t + 1) * 256)
        da_ref[:, cols] = dot_t1(dqkv_ref[...], wi_ref[cols, :])
    gb = gb_ref[...]
    need(x_ref)
    need(dr_ref)
    xhat, rstd = normed(x_ref[...].astype(f32))
    da = da_ref[...]
    e = da * gb[0:1]
    back = rstd * (e - jnp.mean(e, -1, keepdims=True) - xhat * jnp.mean(e * xhat, -1, keepdims=True))
    ig_ref[...] = (dr_ref[...] + back)[:ROWS].astype(bf16)
    tall[...] = jnp.zeros_like(tall)
    tall[0:8, :] = sums_ref[0:8, :]
    tall[0:1, :] = jnp.sum(da * xhat, 0, keepdims=True)
    tall[2:3, :] = jnp.sum(da, 0, keepdims=True)
    tall[4:5, :] = jnp.sum(dqkv_ref[:, :D].astype(f32), 0, keepdims=True)
    tall[5:6, :] = jnp.sum(dqkv_ref[:, 2 * D :].astype(f32), 0, keepdims=True)
    put_rows(y, c, sm_ref, so_ref, tall[...].T.astype(bf16), 0, slice(0, SMALL))
    tall[0:8, :] = sums_ref[8:16, :]
    put_rows(y, c, sm_ref, so_ref, tall[...].T.astype(bf16), 1, slice(0, SMALL))


def kernel_held(im, ir, sm, sr, om, orr, h0, h1, h2, h3, need, flush):
    held = (h0, h1, h2, h3)
    for ref in (im, ir, sm, sr, om, orr):
        need(ref)
    for k in range(NY):
        held[k][:, :1152] = added(im[k], ir[k])
        held[k][:, 1152:1280] = added(sm[k], sr[k])
        held[k][:, 1280:] = added(om[k], orr[k])
        flush(held[k])


def tile_runs():
    runs = []
    for r in range(3):
        col = 0
        while col < 13:
            at = 13 * r + col
            n = min(13 - col, 10 - at % 10)
            runs.append((r, col, at // 10, at % 10, n))
            col += n
    return runs


def kernel_fold(b0, b1, b2, b3, out_ref):
    total = sum(b[...].astype(f32) for b in (b0, b1, b2, b3))
    for zz in range(NZ):
        for r, col, at, place, n in tile_runs():
            rows = slice(zz * SHARD + 8 * r, zz * SHARD + 8 * r + 8)
            block = total[rows, 128 * col : 128 * (col + n)].astype(bf16)
            out_ref[zz * NX + at, :, 128 * place : 128 * (place + n)] = block
        out_ref[zz * NX + 3, :, 1152:] = jnp.zeros((8, 128), bf16)


def kernel_pack(both_ref, up_ref, down_ref, pack_ref, square_ref):
    up = added(*(up_ref[k] for k in range(32)))
    down = added(*(down_ref[k] for k in range(32)))
    both = sum(both_ref[k].astype(f32) for k in range(32))
    both = jnp.concatenate([both[:, :512], both[:, 512:1024], jnp.concatenate(
        [both[:, 1024:], jnp.zeros((8, 256), f32)], 1)], 0).astype(bf16)
    pack_ref[:, :384] = up
    pack_ref[:, 384:768] = down
    pack_ref[:, 768:] = both
    square = sum(jnp.sum(v.astype(f32) * v.astype(f32)) for v in (up, down, both))
    square_ref[...] = jnp.full(square_ref.shape, square, f32)


def kernel_update(pos, square_ref, p0, p1, p2, p3, q0, q1, q2, q3, *refs):
    states, outs, parts = refs[:18], refs[18:-1], refs[-1]
    x, c = pos[2], pos[3]
    square_sum = jnp.sum(square_ref[...]) * (1.0 / 128)
    norm = jnp.sqrt(jnp.full((1, 128), square_sum, f32))
    outs[0][...] = norm
    factor = jnp.minimum(1.0, clip_bound / norm[0:1, 0:1])
    for kx in range(NX):
        at = lax.rem(x - kx + NX, NX)
        for refs_of, core in (((p0, p1, p2, p3), c), ((q0, q1, q2, q3), 1 - c)):
            parts[core * NX + at] = refs_of[kx][...].astype(f32)

    def step(which, grad, rows, cols):
        m, f, s = (r[rows, cols] for r in states[3 * which : 3 * which + 3])
        o = outs[1 + 5 * which : 6 + 5 * which]
        _, weight, mean, square, copy = adam_step(m, f, s, grad, factor)
        o[0][rows, cols] = grad
        o[1][rows, cols] = weight - m if which == 4 else weight
        o[2][rows, cols] = mean
        o[3][rows, cols] = square
        if which != 4:
            o[4][rows, cols] = copy

    every = slice(None)
    smalls = []
    for half in range(2):
        bands = []
        for r in range(3):
            tiles = []
            for col in range(13):
                at, place = divmod(13 * r + col, 10)
                tiles.append(
                    parts[half * NX + at, 8 * (place // 4) : 8 * (place // 4) + 8,
                          768 + 128 * (place % 4) : 896 + 128 * (place % 4)]
                )
            bands.append(jnp.concatenate(tiles, 1))
        grad = jnp.concatenate(bands, 0)
        step(0, grad[:, :1152], every, slice(half * 1152, (half + 1) * 1152))
        smalls.append(grad[:, 1152:1280].T)
        step(1, grad[:, 1280:], every, slice(half * 384, (half + 1) * 384))
        for k in range(NX):
            at = (2 * k + half) * 384
            step(2, parts[half * NX + k, :, :384], every, slice(at, at + 384))
            step(3, parts[half * NX + k, :, 384:768], slice(24 * k, 24 * k + 24), slice(half * 384, (half + 1) * 384))
    lo, hi = smalls
    step(4, lo[0:2], every, every)
    step(5, jnp.concatenate([lo[2:8], hi[0:4]], 0), every, every)


def kernel_block_out(r1_ref, h_ref, wd_ref, gb_ref, out_ref):
    out_ref[...] = (r1_ref[...] + dot(h_ref[...], wd_ref[...]) + gb_ref[7:8])[:ROWS].astype(bf16)


def shift(v, axis, k):
    n = dict(y=NY, z=NZ, x=NX)[axis]
    return lax.ppermute(v, axis, [(i, (i + k) % n) for i in range(n)])


def both_ways(v, axis, k):
    n = dict(y=NY, z=NZ, x=NX)[axis]
    pairs = []
    for i in range(n):
        pairs.append((2 * i, 2 * ((i + k) % n)))
        pairs.append((2 * i + 1, 2 * ((i - k) % n) + 1))
    return lax.ppermute(v, (axis, "c"), pairs)


def swap(v):
    return lax.ppermute(v, "c", [(0, 1), (1, 0)])


def gather4(v, axis):
    return [v] + [shift(v, axis, k) for k in (1, 2, 3)]


def exchange(v, axis):
    return lax.all_to_all(v, axis, split_axis=0, concat_axis=0, tiled=True)


def spread(v, axis, n):
    return exchange(jnp.broadcast_to(v[None], (n,) + v.shape), axis)


def sent4(mine, other, axis):
    got = swap(other)
    held = [added(mine[k], got[k]) for k in range(4)]
    return [held[0]] + [shift(held[k], axis, k) for k in (1, 2, 3)]


def adam_step(master, first, second, grad, factor):
    clipped = grad * factor
    new_first = beta_first * first + (1.0 - beta_first) * clipped
    new_second = beta_second * second + (1.0 - beta_second) * clipped * clipped
    moved = new_first / fix_first / (jnp.sqrt(new_second / fix_second) + adam_eps)
    new_master = master - learn_rate * (moved + decay_rate * master)
    return (grad, new_master, new_first, new_second, new_master.astype(bf16))


def body(
    tokens, episodes, cotangent,
    inproj_master, inproj_first, inproj_second,
    outproj_master, outproj_first, outproj_second,
    upproj_master, upproj_first, upproj_second,
    downproj_master, downproj_first, downproj_second,
    gains_master, gains_first, gains_second,
    biases_master, biases_first, biases_second,
):
    y, z, x, c = (lax.axis_index(a) for a in AXES)
    pos = jnp.stack([y, z, x, c]).astype(jnp.int32)
    tok = jnp.pad(tokens, ((0, PAD - ROWS), (0, 0)))
    cot = jnp.pad(cotangent, ((0, PAD - ROWS), (0, 0)))

    small = jnp.concatenate([gains_master, biases_master], 0).T.astype(bf16)
    small = jnp.pad(small, ((0, 0), (0, SMALL - 12)))
    own = jnp.concatenate([inproj_master.astype(bf16), small, outproj_master.astype(bf16)], 1)
    near = [both_ways(own, "z", k) for k in (1, 2, 3)]
    far = lax.ppermute(own, ("z", "c"), [(2 * i + 1, 2 * ((i + 4) % NZ) + 1) for i in range(NZ)])
    piece = lax.dynamic_slice(upproj_master, (0, (x * 2 + c) * 384), (SHARD, 384)).astype(bf16)
    stack = jnp.stack([jnp.where(c == 0, own, far)] + near)
    stack, tok, cot, pos = lax.optimization_barrier((stack, tok, cot, pos))
    piece, stack = lax.optimization_barrier((piece, stack))
    wu = spread(piece, ("y", "z"), NY * NZ).reshape(D, 384)
    wi_mine = gather4(stack, "y")
    wu, *wi_mine = lax.optimization_barrier((wu, *wi_mine))
    wu_own = jnp.stack([wu, swap(wu)])
    wu_near = both_ways(wu_own, "x", 1)
    wu_far = shift(wu, "x", 2)
    piece = lax.dynamic_slice(downproj_master, (x * SHARD, c * 384), (SHARD, 384)).astype(bf16)
    piece, wu_own = lax.optimization_barrier((piece, wu_own))
    wd = spread(piece, ("y", "z"), NY * NZ).reshape(D, 384)
    wi_other = [swap(v) for v in wi_mine]

    wi, wo, gb, a1, qkv, att, probs, r1, a2 = call(
        kernel_attention,
        [((D, 3 * D), bf16), ((D, D), bf16), ((16, D), f32), ((PAD, D), bf16), ((PAD, 3 * D), bf16), ((PAD, D), bf16),
         ((HEADS, PAD, PAD), bf16), ((PAD, D), f32), ((PAD, D), bf16)],
        [pos, episodes, tok, *wi_mine, *wi_other],
        [((D, 4 * D + SMALL), f32), ((PAD, PAD), f32), ((HEADS, PAD, PAD), bf16)],
        smem=2, early=(0, 1, 3, 4, 5), extra=HEADS // 2, held=(6,),
    )
    wu_near, wu_far, wd, a2 = lax.optimization_barrier((wu_near, wu_far, wd, a2))
    wd_mine = spread(wd, "x", NX).reshape(NX, NY * NZ, SHARD, 384)
    wu, h, g, dm, do = call(
        kernel_up,
        [((D, FF), bf16), ((PAD, FF), bf16), ((PAD, FF), bf16),
         ((NX, NY * NZ, SHARD, 384), bf16), ((NX, NY * NZ, SHARD, 384), bf16)],
        [pos, gb, cot, a2, wu_own, wu_near, swap(wu_near), wu_far, swap(wu_far)],
        late=(4, 5, 6, 7, 8, 2), early=(0, 1, 2),
    )
    wd_mine, h = lax.optimization_barrier((wd_mine, h))
    wd_other = swap(wd_mine)
    wd, um, uo, du, sums = call(
        kernel_down_back,
        [((FF, D), bf16), ((NY, 192, 1536), bf16), ((NY, 192, 1536), bf16), ((PAD, FF), bf16), ((16, D), f32)],
        [pos, cot, g, wd_mine, wd_other, a2],
        late=(1, 2, 5), early=(0, 3),
    )
    down = exchange(added(dm, swap(do)), "x").reshape(NX, D, 384)
    up = sent4(um, uo, "y")
    dr, om, oo, dqkv, sums = call(
        kernel_mid_back,
        [((PAD, D), f32), ((NY, 192, 384), bf16), ((NY, 192, 384), bf16), ((PAD, 3 * D), bf16), ((16, D), f32)],
        [pos, gb, cot, du, wu, r1, sums, att, wo, qkv, probs],
        [((PAD, D), f32), ((PAD, D), bf16), ((PAD, D), bf16), ((HEADS, PAD, PAD), bf16)],
        late=(3, 4, 2, 5, 7, 8, 9), early=(0, 1, 2), extra=HEADS // 2, kept=(10,),
    )
    im, io, down, up = call(
        kernel_in_grad,
        [((NY, 192, 1152), bf16), ((NY, 192, 1152), bf16), ((D, 384), bf16), ((NZ * NX, SHARD, 384), bf16)],
        [pos, dqkv, a1, down, *up],
        late=(3, 4, 5, 6, 7), early=(0, 1, 2),
    )
    down = exchange(down.reshape(NY * NZ, SHARD, 384), ("y", "z"))
    sm, so, input_grad = call(
        kernel_input_grad,
        [((NY, 192, SMALL), bf16), ((NY, 192, SMALL), bf16), ((ROWS, D), bf16)],
        [pos, dqkv, wi, tok, gb, dr, sums],
        [((PAD, D), f32), ((SMALL, D), f32)],
        late=(3, 5),
    )
    both = call(
        kernel_held, [((192, 1664), bf16)] * 4, [im, swap(io), sm, swap(so), om, swap(oo)], smem=0,
        late=(0, 1, 2, 3, 4, 5), early=(0, 1, 2, 3),
    )
    both = [both[0]] + [shift(both[k], "y", k) for k in (1, 2, 3)]
    r1, both[0] = lax.optimization_barrier((r1, both[0]))
    (block_out,) = call(kernel_block_out, [((ROWS, D), bf16)], [r1, h, wd, gb], smem=0, flops=60 * 10**9)
    up, down, block_out = lax.optimization_barrier((up, down, block_out))
    up = exchange(up, ("z", "x"))
    (both,) = call(kernel_fold, [((NZ * NX, 8, 1280), bf16)], both, smem=0)
    both = exchange(both, ("z", "x"))
    pack, square = call(
        kernel_pack, [((SHARD, 1280), bf16), ((256, 128), f32)], [both, up, down], smem=0
    )
    packs = gather4(pack, "x")
    square = exchange(square, AXES)
    packs += [swap(v) for v in packs]
    states = [
        inproj_master, inproj_first, inproj_second,
        outproj_master, outproj_first, outproj_second,
        upproj_master, upproj_first, upproj_second,
        downproj_master, downproj_first, downproj_second,
        gains_master, gains_first, gains_second,
        biases_master, biases_first, biases_second,
    ]
    outs = [((1, 128), f32)]
    for state in states[::3]:
        outs += [(state.shape, f32)] * 4 + [(state.shape, bf16)]
    new = call(kernel_update, outs, [pos, square, *packs, *states], [((NC * NX, SHARD, 1280), f32)])
    norm, new = new[0], new[1:]
    return (block_out, input_grad, norm[0, 0], *new[:24], *new[25:], new[25][5])


def solution(mesh):
    fine = Mesh(mesh.devices.reshape(NY, NZ, NX, NC), AXES)
    rows, own, own_cols = P(AXES, None), P(("y", "z"), None), P(None, ("y", "z"))
    in_specs = (rows, P(AXES), rows) + (own,) * 12 + (own_cols,) * 6
    out_specs = (rows, rows, P()) + (own,) * 20 + (own_cols,) * 9 + (P(("y", "z")),)
    return jax.shard_map(body, mesh=fine, in_specs=in_specs, out_specs=out_specs, check_vma=False)
```
